512 devices in a mesh: blk: 64 (over z, y_hi, x), col: 8 (over y_lo, core).
Axes of the slice: x: 4, y: 8 (y_hi: 2, y_lo: 4; y = y_hi * 4 + y_lo), z: 8, core: 2. Of those that a mesh axis runs over, the one named last changes fastest.
Arguments:
- queries: bfloat16 [512, 16384], P('blk', 'col'), may hold values from -6 to 6
- factor: bfloat16 [16384, 1024], P('col', 'blk'), may hold values from -0.046875 to 0.046875
- eigenvalues: float32 [1024], replicated, may hold values from 0.05 to 20
- damping: float32 [1], replicated, may hold values from 0.5 to 2
- train_rows: bfloat16 [65536, 16384], P('blk', 'col'), may hold values from -0.046875 to 0.046875
Outputs:
- scores: bfloat16 [512, 65536], P('col', 'blk')
The draws below stay inside these ranges and needn't reach their ends.
All inputs are finite; a program needn't handle non-finite values.
Results may differ from the reference program's by a relative error of at most 0.0049.
Values may be sent and summed in bfloat16 or wider, within the bound.
No kernel may reach another device: no remote copies, remote signals or barrier semaphores. Data moves between devices by JAX's collectives and lax.ppermute only.
A program may use at most 64 MiB of HBM per device.

```python
import math
import jax
import jax.numpy as jnp
from jax import lax

PROJ = 16384
RANK = 1024
TR_DEV = 1024
QUERIES = 512
TRAIN = 65536
N_BLK = 64


def block_scale(key, dims, shards, smallest, high):
    loudness = 1.0
    for position, shards_of in shards:
        heights = jax.random.uniform(jax.random.fold_in(jax.random.fold_in(key, 6), position), (shards_of,), jnp.float32, smallest / len(shards), high / len(shards))
        loudness = loudness * jnp.repeat(jnp.exp(heights), dims[position] // shards_of).reshape((-1,) + (1,) * (len(dims) - 1 - position))
    return loudness


def centred(rng, dims, deviation, most, shards=(), dtype=jnp.bfloat16):
    level = block_scale(rng, dims, shards, -0.22, 0.18) if shards else 1.0
    array = jax.random.normal(rng, dims, jnp.float32) * deviation * level
    return jnp.minimum(jnp.maximum(array, -most), most).astype(dtype)


def setup_inputs(seed: int = 0) -> dict:
    key_of = jax.random.split(jax.random.key(seed), 6)
    return {
        "queries": centred(key_of[0], (QUERIES, PROJ), 1.0, 6.0, ((0, 64), (1, 8))),
        "factor": centred(key_of[1], (PROJ, RANK), PROJ ** -0.5, 0.046875, ((0, 8), (1, 64))),
        "eigenvalues": jnp.clip(jnp.exp(jax.random.uniform(key_of[2], (RANK,), jnp.float32, math.log(0.05), math.log(20.0))), 0.05, 20.0),
        "damping": jnp.clip(jnp.exp(jax.random.uniform(key_of[3], (1,), jnp.float32, math.log(0.5), math.log(2.0))), 0.5, 2.0),
        "train_rows": centred(key_of[4], (TRAIN, PROJ), PROJ ** -0.5, 0.046875, ((0, 64), (1, 8))),
    }


def reference(queries, factor, eigenvalues, damping, train_rows):
    damp_value = damping[0]
    weights = eigenvalues / (eigenvalues + damp_value)
    coefficient = jnp.dot(queries, factor, preferred_element_type=jnp.float32)
    scaled = coefficient * weights[None, :]
    correction = jnp.dot(scaled, factor.astype(jnp.float32).T, precision=lax.Precision.HIGHEST)
    preconditioned = ((queries.astype(jnp.float32) - correction) / damp_value).astype(jnp.bfloat16)
    blocks = train_rows.reshape(N_BLK, TR_DEV, PROJ)

    def one_block(block_rows):
        return jnp.dot(preconditioned, block_rows.T, preferred_element_type=jnp.float32).astype(jnp.bfloat16)

    result = lax.map(one_block, blocks)
    return jnp.transpose(result, (1, 0, 2)).reshape(QUERIES, TRAIN)
```

```python
import jax
import jax.numpy as jnp
from jax import lax
from jax.sharding import Mesh
from jax.sharding import PartitionSpec as P

BLK = ("z", "yh", "x")
COL = ("yl", "core")
ROWS = ("z", "yh")


def exchanged(tiles, axes):
    return lax.all_to_all(tiles, axes, 0, 0, tiled=True)


def everyones(shard, axes):
    size = lax.axis_size(axes)
    tiles = exchanged(jnp.broadcast_to(shard[None], (size, *shard.shape)), axes)
    return tiles.reshape(size * shard.shape[0], *shard.shape[1:])


def nt(left, right):
    return lax.dot_general(
        left, right, (((1,), (1,)), ((), ())), preferred_element_type=jnp.float32
    )


def per_device(queries, factor, eigenvalues, damping, train_rows):
    rows, width = queries.shape
    ranks = factor.shape[1]
    cores, n_yl, n_x = lax.axis_size("core"), lax.axis_size("yl"), lax.axis_size("x")
    n_rows = lax.axis_size(ROWS)
    damp_value = damping[0]

    by_x = everyones(queries, "x")
    basis = everyones(factor.T, ROWS)

    mine = lax.dynamic_index_in_dim(
        eigenvalues.reshape(n_rows, n_x, ranks), lax.axis_index("x"), 1, keepdims=False
    ).reshape(-1)
    weights = mine / (mine + damp_value)

    partial_value = nt(by_x, basis)
    size = lax.axis_size(COL)
    coefficient = exchanged(
        jnp.broadcast_to(partial_value[None], (size, *partial_value.shape)), COL
    ).sum(axis=0)
    scaled = coefficient * weights[None, :]
    high = scaled.astype(jnp.bfloat16)
    low = (scaled - high.astype(jnp.float32)).astype(jnp.bfloat16)
    partial_correction = jnp.dot(high, basis, preferred_element_type=jnp.float32) + jnp.dot(
        low, basis, preferred_element_type=jnp.float32
    )
    terms = exchanged(
        partial_correction.astype(jnp.bfloat16).reshape(n_x, rows, width), "x"
    )
    correction = terms.astype(jnp.float32).sum(axis=0)
    pre_own = ((queries.astype(jnp.float32) - correction) / damp_value).astype(jnp.bfloat16)

    pre_rows = everyones(pre_own, ROWS)
    pre = everyones(pre_rows, "x")
    partial_scores = nt(pre, train_rows).reshape(n_x, n_yl, cores, -1, train_rows.shape[0])
    core = lax.axis_index("core")
    kept = lax.dynamic_index_in_dim(partial_scores, core, 2, keepdims=False)
    sent = lax.dynamic_index_in_dim(partial_scores, 1 - core, 2, keepdims=False)
    came = lax.ppermute(sent.astype(jnp.bfloat16), "core", [(0, 1), (1, 0)])
    pair = (kept + came.astype(jnp.float32)).astype(jnp.bfloat16)
    parts = exchanged(pair.transpose(1, 0, 2, 3), "yl")
    scores = parts.astype(jnp.float32).sum(axis=0)
    n_yh = lax.axis_size("yh")
    scores = scores.reshape(n_x, n_yh, rows, -1).transpose(1, 0, 2, 3)
    return scores.astype(jnp.bfloat16).reshape(n_x * n_yh * rows, -1)


def solution(mesh):
    split = Mesh(mesh.devices.reshape(8, 2, 4, 4, 2), BLK + COL)
    in_specs = (P(BLK, COL), P(COL, BLK), P(), P(), P(BLK, COL))
    out_specs = P(COL, BLK)
    return jax.shard_map(
        per_device, mesh=split, in_specs=in_specs, out_specs=out_specs, check_vma=False
    )
```

```python
import jax
import jax.numpy as jnp
from jax import lax
from jax.sharding import Mesh
from jax.sharding import PartitionSpec as P

BLK = ("z", "yh", "x")
COL = ("yl", "core")
ROWS = ("z", "yh")
PLANE = ("x", "yh")


def exchanged(tiles, axes):
    return lax.all_to_all(tiles, axes, 0, 0, tiled=True)


def everyones(shard, axes):
    size = lax.axis_size(axes)
    tiles = exchanged(jnp.broadcast_to(shard[None], (size, *shard.shape)), axes)
    return tiles.reshape(size * shard.shape[0], *shard.shape[1:])


def from_next(shard, axis, step):
    size = lax.axis_size(axis)
    return lax.ppermute(shard, axis, [((i + step) % size, i) for i in range(size)])


def nt(left, right):
    return lax.dot_general(
        left, right, (((1,), (1,)), ((), ())), preferred_element_type=jnp.float32
    )


def per_device(queries, factor, eigenvalues, damping, train_rows):
    rows, width = queries.shape
    ranks = factor.shape[1]
    n_x, n_z = lax.axis_size("x"), lax.axis_size("z")
    x, core = lax.axis_index("x"), lax.axis_index("core")
    damp_value = damping[0]

    basis = everyones(factor.T, "z")
    near = everyones(queries, PLANE)

    mine = lax.dynamic_index_in_dim(
        eigenvalues.reshape(n_z, -1, ranks), lax.axis_index(("yh", "x")), 1, keepdims=False
    ).reshape(-1)
    weights = mine / (mine + damp_value)

    partial_value = nt(near, basis).astype(jnp.bfloat16)
    coefficient = everyones(partial_value[None], COL).astype(jnp.float32).sum(axis=0)
    scaled = coefficient * weights[None, :]
    partial_correction = jnp.dot(
        scaled.astype(jnp.bfloat16), basis, preferred_element_type=jnp.float32
    )
    terms = exchanged(
        partial_correction.astype(jnp.bfloat16).reshape(-1, rows, width), PLANE
    )
    correction = terms.astype(jnp.float32).sum(axis=0)
    pre_own = ((queries.astype(jnp.float32) - correction) / damp_value).astype(jnp.bfloat16)

    chunk = everyones(pre_own, ROWS)
    half = chunk.shape[0] // 2
    after = from_next(chunk, "x", 1)
    before = from_next(chunk, "x", n_x - 1)
    far_after = from_next(after[:half], "x", 1)
    far_before = from_next(before[half:], "x", n_x - 1)

    def reduced_on_chip(blocks):
        value = nt(jnp.concatenate(blocks, 0), train_rows)
        value = value.reshape(-1, lax.axis_size("yl"), 2, chunk.shape[0] // n_z, train_rows.shape[0])
        kept = lax.dynamic_index_in_dim(value, core, 2, keepdims=False)
        sent = lax.dynamic_index_in_dim(value, 1 - core, 2, keepdims=False)
        came = lax.ppermute(sent.astype(jnp.bfloat16), "core", [(0, 1), (1, 0)])
        return (kept + came.astype(jnp.float32)).astype(jnp.bfloat16)

    first = reduced_on_chip((chunk, after, before))
    last = reduced_on_chip((far_after, far_before))
    pair = jnp.concatenate([first[:2], last, first[2:]], 0)
    parts = exchanged(pair.transpose(1, 0, 2, 3), "yl")
    scores = parts.astype(jnp.float32).sum(axis=0).astype(jnp.bfloat16)
    scores = lax.dynamic_slice_in_dim(jnp.concatenate([scores, scores], 0), n_x - x, n_x)
    n_yh = lax.axis_size("yh")
    scores = scores.reshape(n_x, n_yh, rows, -1).transpose(1, 0, 2, 3)
    return scores.reshape(n_x * n_yh * rows, -1)


def solution(mesh):
    split = Mesh(mesh.devices.reshape(8, 2, 4, 4, 2), BLK + COL)
    in_specs = (P(BLK, COL), P(COL, BLK), P(), P(), P(BLK, COL))
    out_specs = P(COL, BLK)
    return jax.shard_map(
        per_device, mesh=split, in_specs=in_specs, out_specs=out_specs, check_vma=False
    )
```

```python
import jax
import jax.numpy as jnp
from jax import lax
from jax.sharding import Mesh
from jax.sharding import PartitionSpec as P

BLK = ("z", "yh", "x")
COL = ("yl", "core")
ROWS = ("z", "yh")
PLANE = ("x", "yh")


def exchanged(tiles, axes):
    return lax.all_to_all(tiles, axes, 0, 0, tiled=True)


def everyones(shard, axes):
    size = lax.axis_size(axes)
    tiles = exchanged(jnp.broadcast_to(shard[None], (size, *shard.shape)), axes)
    return tiles.reshape(size * shard.shape[0], *shard.shape[1:])


def from_next(shard, axis, step):
    size = lax.axis_size(axis)
    return lax.ppermute(shard, axis, [((i + step) % size, i) for i in range(size)])


def nt(left, right):
    return lax.dot_general(
        left, right, (((1,), (1,)), ((), ())), preferred_element_type=jnp.float32
    )


def per_device(queries, factor, eigenvalues, damping, train_rows):
    rows, width = queries.shape
    ranks = factor.shape[1]
    n_x, n_z = lax.axis_size("x"), lax.axis_size("z")
    x, core = lax.axis_index("x"), lax.axis_index("core")
    damp_value = damping[0]

    own = factor.T
    other = lax.ppermute(own, "yh", [(0, 1), (1, 0)])
    near = everyones(queries, "z")
    other = other + near[:ranks] * 0
    both = jnp.concatenate([own, other], 0)
    basis = everyones(both, "x").reshape(-1, width)

    mine = lax.dynamic_index_in_dim(
        eigenvalues.reshape(n_z, -1), lax.axis_index("z"), 0, keepdims=False
    ).reshape(-1, n_x, ranks)
    mine = jnp.where(lax.axis_index("yh") == 0, mine, mine[::-1]).transpose(1, 0, 2).reshape(-1)
    weights = mine / (mine + damp_value)

    partial_value = nt(near, basis).astype(jnp.bfloat16)
    coefficient = everyones(partial_value[None], COL).astype(jnp.float32).sum(axis=0)
    scaled = coefficient * weights[None, :]
    partial_correction = jnp.dot(
        scaled.astype(jnp.bfloat16), basis, preferred_element_type=jnp.float32
    )
    terms = exchanged(
        partial_correction.astype(jnp.bfloat16).reshape(-1, rows, width), "z"
    )
    correction = terms.astype(jnp.float32).sum(axis=0)
    pre_own = ((queries.astype(jnp.float32) - correction) / damp_value).astype(jnp.bfloat16)

    chunk = everyones(pre_own, ROWS)
    half = chunk.shape[0] // 2
    after = from_next(chunk, "x", 1)
    before = from_next(chunk, "x", n_x - 1)
    far_after = from_next(after[:half], "x", 1)
    far_before = from_next(before[half:], "x", n_x - 1)

    def reduced_on_chip(blocks):
        value = nt(jnp.concatenate(blocks, 0), train_rows)
        value = value.reshape(-1, lax.axis_size("yl"), 2, chunk.shape[0] // n_z, train_rows.shape[0])
        kept = lax.dynamic_index_in_dim(value, core, 2, keepdims=False)
        sent = lax.dynamic_index_in_dim(value, 1 - core, 2, keepdims=False)
        came = lax.ppermute(sent.astype(jnp.bfloat16), "core", [(0, 1), (1, 0)])
        return (kept + came.astype(jnp.float32)).astype(jnp.bfloat16)

    first = reduced_on_chip((chunk, after, before))
    last = reduced_on_chip((far_after, far_before))
    pair = jnp.concatenate([first[:2], last, first[2:]], 0)
    parts = exchanged(pair.transpose(1, 0, 2, 3), "yl")
    scores = parts.astype(jnp.float32).sum(axis=0).astype(jnp.bfloat16)
    scores = lax.dynamic_slice_in_dim(jnp.concatenate([scores, scores], 0), n_x - x, n_x)
    n_yh = lax.axis_size("yh")
    scores = scores.reshape(n_x, n_yh, rows, -1).transpose(1, 0, 2, 3)
    return scores.reshape(n_x * n_yh * rows, -1)


def solution(mesh):
    split = Mesh(mesh.devices.reshape(8, 2, 4, 4, 2), BLK + COL)
    in_specs = (P(BLK, COL), P(COL, BLK), P(), P(), P(BLK, COL))
    out_specs = P(COL, BLK)
    return jax.shard_map(
        per_device, mesh=split, in_specs=in_specs, out_specs=out_specs, check_vma=False
    )
```

```python
import jax
import jax.numpy as jnp
from jax import lax
from jax.experimental import pallas as pl
from jax.experimental.pallas import tpu as pltpu
from jax.sharding import Mesh
from jax.sharding import PartitionSpec as P

BLK = ("z", "yh", "x")
COL = ("yl", "core")
ROWS = ("z", "yh")
PLANE = ("x", "yh")


def exchanged(tiles, axes):
    return lax.all_to_all(tiles, axes, 0, 0, tiled=True)


def everyones(shard, axes):
    size = lax.axis_size(axes)
    tiles = exchanged(jnp.broadcast_to(shard[None], (size, *shard.shape)), axes)
    return tiles.reshape(size * shard.shape[0], *shard.shape[1:])


def from_next(shard, axis, step):
    size = lax.axis_size(axis)
    return lax.ppermute(shard, axis, [((i + step) % size, i) for i in range(size)])


def nt(left, right):
    return lax.dot_general(
        left, right, (((1,), (1,)), ((), ())), preferred_element_type=jnp.float32
    )


def chunk_scores(blocks, train_rows, core, run):
    total = sum(b.shape[0] for b in blocks)
    groups, (n_train, width) = total // (2 * run), train_rows.shape
    step = 256

    def kernel(core_ref, *refs):
        block_refs, (train_ref, kept_ref, sent_ref) = refs[:-3], refs[-3:]
        left = jnp.concatenate([r[...] for r in block_refs], 0)
        first = core_ref[0] == 0
        for start in range(0, n_train, step):
            value = nt(left, train_ref[start : start + step, :]).reshape(groups, 2, run, step)
            low, high = value[:, 0], value[:, 1]
            kept_ref[:, :, start : start + step] = jnp.where(first, low, high)
            sent_ref[:, :, start : start + step] = jnp.where(first, high, low).astype(jnp.bfloat16)

    vmem = pl.BlockSpec(memory_space=pltpu.VMEM)
    return pl.pallas_call(
        kernel,
        out_shape=(
            jax.ShapeDtypeStruct((groups, run, n_train), jnp.float32),
            jax.ShapeDtypeStruct((groups, run, n_train), jnp.bfloat16),
        ),
        in_specs=[pl.BlockSpec(memory_space=pltpu.SMEM)] + [vmem] * (len(blocks) + 1),
        out_specs=(vmem, vmem),
        compiler_params=pltpu.CompilerParams(vmem_limit_bytes=16 * 1024 * 1024),
        cost_estimate=pl.CostEstimate(
            flops=12 * total * n_train * width,
            bytes_accessed=2 * (total + n_train) * width + 3 * total * n_train,
            transcendentals=0,
        ),
    )(core.reshape(1).astype(jnp.int32), *blocks, train_rows)


def per_device(queries, factor, eigenvalues, damping, train_rows):
    rows, width = queries.shape
    ranks = factor.shape[1]
    n_x, n_z = lax.axis_size("x"), lax.axis_size("z")
    x, core = lax.axis_index("x"), lax.axis_index("core")
    damp_value = damping[0]

    own = factor.T
    other = lax.ppermute(own, "yh", [(0, 1), (1, 0)])
    near = everyones(queries, "z")
    other = other + near[:ranks] * 0
    both = jnp.concatenate([own, other], 0)
    basis = everyones(both, "x").reshape(-1, width)

    mine = lax.dynamic_index_in_dim(
        eigenvalues.reshape(n_z, -1), lax.axis_index("z"), 0, keepdims=False
    ).reshape(-1, n_x, ranks)
    mine = jnp.where(lax.axis_index("yh") == 0, mine, mine[::-1]).transpose(1, 0, 2).reshape(-1)
    weights = mine / (mine + damp_value)

    partial_value = nt(near, basis).astype(jnp.bfloat16)
    coefficient = everyones(partial_value[None], COL).astype(jnp.float32).sum(axis=0)
    scaled = coefficient * weights[None, :]
    partial_correction = jnp.dot(
        scaled.astype(jnp.bfloat16), basis, preferred_element_type=jnp.float32
    )
    terms = exchanged(
        partial_correction.astype(jnp.bfloat16).reshape(-1, rows, width), "z"
    )
    correction = terms.astype(jnp.float32).sum(axis=0)
    pre_own = ((queries.astype(jnp.float32) - correction) / damp_value).astype(jnp.bfloat16)

    chunk = everyones(pre_own, ROWS)
    half = chunk.shape[0] * 5 // 8
    after = from_next(chunk, "x", 1)
    before = from_next(chunk, "x", n_x - 1)
    far_after = from_next(after[:half], "x", 1)
    far_before = from_next(before[half:], "x", n_x - 1)

    def reduced_on_chip(blocks):
        kept, sent = chunk_scores(blocks, train_rows, core, chunk.shape[0] // n_z)
        came = lax.ppermute(sent, "core", [(0, 1), (1, 0)])
        value = (kept + came.astype(jnp.float32)).astype(jnp.bfloat16)
        return value.reshape(-1, lax.axis_size("yl"), *value.shape[1:])

    first = reduced_on_chip((chunk, after, before))
    last = reduced_on_chip((far_after, far_before))
    pair = jnp.concatenate([first[:2], last, first[2:]], 0)
    parts = exchanged(pair.transpose(1, 0, 2, 3), "yl")
    scores = parts.astype(jnp.float32).sum(axis=0).astype(jnp.bfloat16)
    scores = lax.dynamic_slice_in_dim(jnp.concatenate([scores, scores], 0), n_x - x, n_x)
    n_yh = lax.axis_size("yh")
    scores = scores.reshape(n_x, n_yh, rows, -1).transpose(1, 0, 2, 3)
    return scores.reshape(n_x * n_yh * rows, -1)


def solution(mesh):
    split = Mesh(mesh.devices.reshape(8, 2, 4, 4, 2), BLK + COL)
    in_specs = (P(BLK, COL), P(COL, BLK), P(), P(), P(BLK, COL))
    out_specs = P(COL, BLK)
    return jax.shard_map(
        per_device, mesh=split, in_specs=in_specs, out_specs=out_specs, check_vma=False
    )
```

```python
import jax
import jax.numpy as jnp
from jax import lax
from jax.experimental import pallas as pl
from jax.experimental.pallas import tpu as pltpu
from jax.sharding import Mesh
from jax.sharding import PartitionSpec as P

BLK = ("z", "yh", "x")
COL = ("yl", "core")
ROWS = ("z", "yh")
PLANE = ("x", "yh")


def exchanged(tiles, axes):
    return lax.all_to_all(tiles, axes, 0, 0, tiled=True)


def everyones(shard, axes):
    size = lax.axis_size(axes)
    tiles = exchanged(jnp.broadcast_to(shard[None], (size, *shard.shape)), axes)
    return tiles.reshape(size * shard.shape[0], *shard.shape[1:])


def from_next(shard, axis, step):
    size = lax.axis_size(axis)
    return lax.ppermute(shard, axis, [((i + step) % size, i) for i in range(size)])


def nt(left, right):
    return lax.dot_general(
        left, right, (((1,), (1,)), ((), ())), preferred_element_type=jnp.float32
    )


def chunk_scores(blocks, train_rows, core, run):
    total = sum(b.shape[0] for b in blocks)
    groups, (n_train, width) = total // (2 * run), train_rows.shape
    step = 256

    def kernel(core_ref, *refs):
        block_refs, (train_ref, kept_ref, sent_ref) = refs[:-3], refs[-3:]
        left = jnp.concatenate([r[...] for r in block_refs], 0)
        first = core_ref[0] == 0
        for start in range(0, n_train, step):
            value = nt(left, train_ref[start : start + step, :]).reshape(groups, 2, run, step)
            low, high = value[:, 0], value[:, 1]
            kept_ref[:, :, start : start + step] = jnp.where(first, low, high)
            sent_ref[:, :, start : start + step] = jnp.where(first, high, low).astype(jnp.bfloat16)

    vmem = pl.BlockSpec(memory_space=pltpu.VMEM)
    return pl.pallas_call(
        kernel,
        out_shape=(
            jax.ShapeDtypeStruct((groups, run, n_train), jnp.float32),
            jax.ShapeDtypeStruct((groups, run, n_train), jnp.bfloat16),
        ),
        in_specs=[pl.BlockSpec(memory_space=pltpu.SMEM)] + [vmem] * (len(blocks) + 1),
        out_specs=(vmem, vmem),
        compiler_params=pltpu.CompilerParams(vmem_limit_bytes=16 * 1024 * 1024),
        cost_estimate=pl.CostEstimate(
            flops=12 * total * n_train * width,
            bytes_accessed=2 * (total + n_train) * width + 3 * total * n_train,
            transcendentals=0,
        ),
    )(core.reshape(1).astype(jnp.int32), *blocks, train_rows)


def repeated_pair(top, bottom, copies, after):
    def kernel(top_ref, bottom_ref, _, out_ref):
        both = jnp.concatenate([top_ref[...], bottom_ref[...]], 0)
        for i in range(copies):
            out_ref[i] = both

    vmem = pl.BlockSpec(memory_space=pltpu.VMEM)
    shape = (copies, top.shape[0] + bottom.shape[0], top.shape[1])
    return pl.pallas_call(
        kernel,
        out_shape=jax.ShapeDtypeStruct(shape, top.dtype),
        in_specs=[vmem, vmem, pl.BlockSpec(memory_space=pl.ANY)],
        out_specs=vmem,
        compiler_params=pltpu.CompilerParams(vmem_limit_bytes=12 * 1024 * 1024),
    )(top, bottom, after)


def per_device(queries, factor, eigenvalues, damping, train_rows):
    rows, width = queries.shape
    ranks = factor.shape[1]
    n_x, n_z = lax.axis_size("x"), lax.axis_size("z")
    x, core = lax.axis_index("x"), lax.axis_index("core")
    damp_value = damping[0]

    own = factor.T
    other = lax.ppermute(own, "yh", [(0, 1), (1, 0)])
    near = everyones(queries, "z")
    held = own + queries[:1] * 0
    basis = exchanged(repeated_pair(held, other, n_x, near), "x").reshape(-1, width)

    mine = lax.dynamic_index_in_dim(
        eigenvalues.reshape(n_z, -1), lax.axis_index("z"), 0, keepdims=False
    ).reshape(-1, n_x, ranks)
    mine = jnp.where(lax.axis_index("yh") == 0, mine, mine[::-1]).transpose(1, 0, 2).reshape(-1)
    weights = mine / (mine + damp_value)

    partial_value = nt(near, basis).astype(jnp.bfloat16)
    coefficient = everyones(partial_value[None], COL).astype(jnp.float32).sum(axis=0)
    scaled = coefficient * weights[None, :]
    partial_correction = jnp.dot(
        scaled.astype(jnp.bfloat16), basis, preferred_element_type=jnp.float32
    )
    terms = exchanged(
        partial_correction.astype(jnp.bfloat16).reshape(-1, rows, width), "z"
    )
    correction = terms.astype(jnp.float32).sum(axis=0)
    pre_own = ((queries.astype(jnp.float32) - correction) / damp_value).astype(jnp.bfloat16)

    chunk = everyones(pre_own, ROWS)
    half = chunk.shape[0] * 5 // 8
    after = from_next(chunk, "x", 1)
    before = from_next(chunk, "x", n_x - 1)
    far_after = from_next(after[:half], "x", 1)
    far_before = from_next(before[half:], "x", n_x - 1)

    def reduced_on_chip(blocks):
        kept, sent = chunk_scores(blocks, train_rows, core, chunk.shape[0] // n_z)
        came = lax.ppermute(sent, "core", [(0, 1), (1, 0)])
        value = (kept + came.astype(jnp.float32)).astype(jnp.bfloat16)
        return value.reshape(-1, lax.axis_size("yl"), *value.shape[1:])

    first = reduced_on_chip((chunk, after, before))
    last = reduced_on_chip((far_after, far_before))
    pair = jnp.concatenate([first[:2], last, first[2:]], 0)
    parts = exchanged(pair.transpose(1, 0, 2, 3), "yl")
    scores = parts.astype(jnp.float32).sum(axis=0).astype(jnp.bfloat16)
    scores = lax.dynamic_slice_in_dim(jnp.concatenate([scores, scores], 0), n_x - x, n_x)
    n_yh = lax.axis_size("yh")
    scores = scores.reshape(n_x, n_yh, rows, -1).transpose(1, 0, 2, 3)
    return scores.reshape(n_x * n_yh * rows, -1)


def solution(mesh):
    split = Mesh(mesh.devices.reshape(8, 2, 4, 4, 2), BLK + COL)
    in_specs = (P(BLK, COL), P(COL, BLK), P(), P(), P(BLK, COL))
    out_specs = P(COL, BLK)
    return jax.shard_map(
        per_device, mesh=split, in_specs=in_specs, out_specs=out_specs, check_vma=False
    )
```
